32 devices in a mesh: pts: 32 (over z, y, x, core), rank: 1.
Axes of the slice: x: 2, y: 2, z: 4, core: 2. Of those that a mesh axis runs over, the one named last changes fastest.
Arguments:
- points: bfloat16 [32768, 256], P('pts', 'rank'), may hold values from -6 to 6
- prior: float32 [32768, 1024], P('pts', 'rank'), may hold values from -0.125 to 0.125
- first_pivots: int32 [256], replicated, may hold values from 0 to 32767, as said below
- second_pivots: int32 [256], replicated, may hold values from 0 to 32767, as said below
Outputs:
- first_columns: float32 [32768, 256], P('pts', 'rank')
- second_columns: float32 [32768, 256], P('pts', 'rank')
The draws below stay inside these ranges and needn't reach their ends.
Inputs may be any that keep to these rules, and one draw needn't show every extreme that they name: `first_pivots`: the 256 entries are distinct, and none of them is in second_pivots. `second_pivots`: the 256 entries are distinct, and none of them is in first_pivots.
All inputs are finite; a program needn't handle non-finite values.
Results may differ from the reference program's by a relative error of at most 0.0003.
Values sent between devices are 32-bit elements; how exact they have to be, the bound alone decides.
A program may use at most 64 MiB of HBM per device.

```python
import jax
import jax.numpy as jnp
from jax import lax

DF = 256
R0 = 1024
B = 256
NPTS = 32768


def pivot_pair(key):
    folded = jax.random.fold_in(key, 11)
    subkeys = jax.random.split(folded, 3)
    middle = 1 + jax.random.permutation(subkeys[0], NPTS - 2)[:2 * B - 2].astype(jnp.int32)
    leading = jnp.concatenate([jnp.array([NPTS - 1], dtype=jnp.int32), middle[:B - 1]])
    trailing = jnp.concatenate([jnp.array([0], dtype=jnp.int32), middle[B - 1:]])
    leading = jnp.roll(leading, jax.random.randint(subkeys[1], (), 0, B))
    trailing = jnp.roll(trailing, jax.random.randint(subkeys[2], (), 0, B))
    return (leading, trailing)


def draw_first_pivots(key, part):
    return pivot_pair(key)[0]


def draw_second_pivots(key, part):
    return pivot_pair(key)[1]


def block_scale(stream_key, shape, cuts, low, top_value):
    level, own = 1.0, jax.random.fold_in(stream_key, 6)
    for dim, shards_of in cuts:
        draws = jnp.exp(jax.random.uniform(jax.random.fold_in(own, dim), (shards_of,), jnp.float32, low / len(cuts), top_value / len(cuts)))
        level = level * jnp.repeat(draws, shape[dim] // shards_of).reshape([-1 if axis == dim else 1 for axis in range(len(shape))])
    return level


def scatter_about(own_key, shape, spread, most, cuts=(), held_as=jnp.bfloat16):
    factor_of = block_scale(own_key, shape, cuts, -0.22, 0.18) if cuts else 1.0
    result = jax.random.normal(own_key, shape, jnp.float32) * spread * factor_of
    return jnp.minimum(jnp.maximum(result, -most), most).astype(held_as)


def setup_inputs(seed: int = 0) -> dict:
    keys = jax.random.split(jax.random.key(seed), 5)
    return {
        "points": scatter_about(keys[0], (NPTS, DF), 1.0, 6.0, ((0, 32),)),
        "prior": scatter_about(keys[1], (NPTS, R0), (2 * R0) ** -0.5, 0.125, ((0, 32),), jnp.float32),
        "first_pivots": draw_first_pivots(jax.random.fold_in(keys[4], 71), 0),
        "second_pivots": draw_second_pivots(jax.random.fold_in(keys[4], 71), 0),
    }


NUGGET = 2.0

def contract(left_rows, right_rows):
    return lax.dot_general(left_rows.astype(jnp.float32), right_rows.astype(jnp.float32), (((1,), (1,)), ((), ())), precision=lax.Precision.HIGHEST, preferred_element_type=jnp.float32)

def kernel_panel(points, row_norms, prior, pivots):
    piv_x = jnp.take(points, pivots, axis=0)
    cross = lax.dot_general(points.astype(jnp.float32), piv_x.astype(jnp.float32), (((1,), (1,)), ((), ())), preferred_element_type=jnp.float32)
    distance = row_norms[:, None] + jnp.take(row_norms, pivots)[None, :] - 2.0 * cross
    global_ids = jnp.arange(points.shape[0], dtype=jnp.int32)
    matches = (global_ids[:, None] == pivots[None, :]).astype(jnp.float32)
    return jnp.exp(-distance / DF) + NUGGET * matches - contract(prior, jnp.take(prior, pivots, axis=0))

def inverse_factor(kernel_block):
    lower_factor = jnp.linalg.cholesky(kernel_block)
    identity = jnp.eye(kernel_block.shape[0], dtype=jnp.float32)
    return jax.scipy.linalg.solve_triangular(lower_factor, identity, lower=True)

def reference(points, prior, first_pivots, second_pivots):
    wide = points.astype(jnp.float32)
    row_norms = jnp.sum(wide * wide, axis=1)
    first_panel = kernel_panel(points, row_norms, prior, first_pivots)
    first_inverse = inverse_factor(jnp.take(first_panel, first_pivots, axis=0))
    first_columns = contract(first_panel, first_inverse)
    second_panel = kernel_panel(points, row_norms, prior, second_pivots) - contract(first_columns, jnp.take(first_columns, second_pivots, axis=0))
    second_inverse = inverse_factor(jnp.take(second_panel, second_pivots, axis=0))
    second_columns = contract(second_panel, second_inverse)
    return (first_columns, second_columns)
```

```python
import functools

import jax
import jax.numpy as jnp
from jax import lax
from jax.experimental import pallas as pl
from jax.experimental.pallas import tpu as pltpu
from jax.sharding import PartitionSpec as P

NUGGET = 2.0
LANES = 128
GROUP = 8
MIB = 1 << 20


def contract(left_rows, right_rows, precision=None):
    return lax.dot_general(
        left_rows,
        right_rows,
        (((1,), (1,)), ((), ())),
        precision=precision,
        preferred_element_type=jnp.float32,
    )


def owned_rows(source, pivots, first_id):
    row_count = source.shape[0]
    local_index = pivots - first_id
    inside = (local_index >= 0) & (local_index < row_count)
    picked = jnp.take(source, jnp.clip(local_index, 0, row_count - 1), axis=0)
    return jnp.where(inside[:, None], picked.astype(jnp.float32), 0.0)


def square_norms(values):
    wide = values.astype(jnp.float32)
    return jnp.sum(wide * wide, axis=1)


def chain_plan(bits, columns):
    tiles = columns // LANES
    middle = list(range(1, bits - 1))
    ways = max(1, min(len(middle), 3, tiles))
    edges = [LANES * (tiles * way // ways) for way in range(ways + 1)]
    plan = []
    for way in range(ways):
        order = [0] + middle[way:] + middle[:way] + [bits - 1]
        plan.append((order, edges[way], edges[way + 1]))
    return plan


def exchange_kernel(bits, plan, mine_ref, sum_ref, work, landed, send_sem, recv_sem):
    me, rank = lax.axis_index("pts"), lax.axis_index("rank")
    rows = sum_ref.shape[0]
    half_of = [(me // (1 << b)) % 2 for b in range(bits)]
    partner_of = [me + (1 - 2 * half_of[b]) * (1 << b) for b in range(bits)]

    barrier = pltpu.get_barrier_semaphore()
    for b in range(bits):
        pl.semaphore_signal(
            barrier, inc=1, device_id=(partner_of[b], rank), device_id_type=pl.DeviceIdType.MESH
        )
    pl.semaphore_wait(barrier, bits)

    def copy(source, target, b, step, way):
        return pltpu.make_async_remote_copy(
            src_ref=source,
            dst_ref=target,
            send_sem=send_sem.at[step, way],
            recv_sem=recv_sem.at[step, way],
            device_id=(partner_of[b], rank),
            device_id_type=pl.DeviceIdType.MESH,
        )

    starts = [0 for _ in plan]
    running = [None for _ in plan]
    unit = rows >> bits

    def begin_halving(way, step):
        order, left, right = plan[way]
        b, size = order[step], rows >> (step + 1)
        offset = rows - (rows >> step)
        away = pl.multiple_of(starts[way] + (1 - half_of[b]) * size, unit)
        source = work if step else mine_ref
        running[way] = copy(
            source.at[pl.ds(away, size), pl.ds(left, right - left)],
            landed.at[pl.ds(offset, size), pl.ds(left, right - left)],
            b, step, way,
        )
        running[way].start()

    def end_halving(way, step):
        order, left, right = plan[way]
        b, size = order[step], rows >> (step + 1)
        offset = rows - (rows >> step)
        running[way].wait()
        starts[way] = starts[way] + half_of[b] * size
        keep = pl.ds(pl.multiple_of(starts[way], unit), size)
        source = work if step else mine_ref
        target = work if step < bits - 1 else sum_ref
        target[keep, left:right] = source[keep, left:right] + landed[offset:offset + size, left:right]

    def begin_doubling(way, step):
        order, left, right = plan[way]
        b, size = order[step], rows >> (step + 1)
        block = sum_ref.at[pl.ds(pl.multiple_of(starts[way], unit), size), pl.ds(left, right - left)]
        running[way] = copy(block, block, b, 2 * bits - 1 - step, way)
        running[way].start()

    def end_doubling(way, step):
        order, left, right = plan[way]
        b, size = order[step], rows >> (step + 1)
        running[way].wait()
        starts[way] = starts[way] - half_of[b] * size

    ways = range(len(plan))
    for way in ways:
        begin_halving(way, 0)
    for step in range(bits):
        for way in ways:
            end_halving(way, step)
            if step < bits - 1:
                begin_halving(way, step + 1)
            else:
                begin_doubling(way, step)
    for step in reversed(range(bits)):
        for way in ways:
            end_doubling(way, step)
            if step > 0:
                begin_doubling(way, step - 1)


def sum_over_points(mine):
    count = lax.axis_size("pts")
    rows, columns = mine.shape
    bits = count.bit_length() - 1
    if count != 1 << bits or bits < 3 or rows % (8 * count) or columns % LANES:
        return lax.psum(mine, "pts")
    plan = chain_plan(bits, columns)
    return pl.pallas_call(
        functools.partial(exchange_kernel, bits, plan),
        out_shape=jax.ShapeDtypeStruct(mine.shape, jnp.float32),
        in_specs=[pl.BlockSpec(memory_space=pltpu.VMEM)],
        out_specs=pl.BlockSpec(memory_space=pltpu.VMEM),
        scratch_shapes=[
            pltpu.VMEM((rows, columns), jnp.float32),
            pltpu.VMEM((rows, columns), jnp.float32),
            pltpu.SemaphoreType.DMA((2 * bits, len(plan))),
            pltpu.SemaphoreType.DMA((2 * bits, len(plan))),
        ],
        compiler_params=pltpu.CompilerParams(
            collective_id=0, has_side_effects=True, vmem_limit_bytes=24 * MIB
        ),
    )(mine)


def invert_diagonal(tiles):
    count = len(tiles)
    tiles = list(tiles)
    sub = lax.broadcasted_iota(jnp.int32, (GROUP, LANES), 0)
    lane = lax.broadcasted_iota(jnp.int32, (GROUP, LANES), 1)
    result = []
    for g in range(count):
        base = g * GROUP
        rows = tiles[g]
        cols = [jnp.broadcast_to(rows[:, base + k:base + k + 1], (GROUP, LANES)) for k in range(GROUP)]
        in_group = (lane >= base) & (lane < base + GROUP)
        rows = jnp.where(in_group, jnp.where(lane == sub + base, 1.0, 0.0), rows)
        scale = jnp.zeros((GROUP, LANES), jnp.float32)
        for k in range(GROUP):
            inv = 1.0 / jnp.broadcast_to(cols[k][k:k + 1, :], (GROUP, LANES))
            scale = jnp.where(sub == k, inv, scale)
            if k < GROUP - 1:
                mult = jnp.where(sub > k, cols[k] * inv, 0.0)
                for j in range(k + 1, GROUP):
                    cols[j] = cols[j] - mult * jnp.broadcast_to(cols[j][k:k + 1, :], (GROUP, LANES))
                rows = rows - mult * jnp.broadcast_to(rows[k:k + 1, :], (GROUP, LANES))
        result.append(jnp.where(lane <= sub + base, rows * jnp.sqrt(scale), 0.0))
        if g < count - 1:
            across = jnp.transpose(rows * scale)
            spread = [jnp.broadcast_to(rows[k:k + 1, :], (GROUP, LANES)) for k in range(GROUP)]
            for i in range(g + 1, count):
                part = across[i * GROUP:(i + 1) * GROUP, :]
                tile = jnp.where(in_group, 0.0, tiles[i])
                for k in range(GROUP):
                    tile = tile - jnp.broadcast_to(part[:, k:k + 1], (GROUP, LANES)) * spread[k]
                tiles[i] = tile
    return result


def inverse_kernel(a_ref, w_ref, work):
    size = a_ref.shape[0]
    blocks = size // LANES
    exact = lax.Precision.HIGHEST
    work[...] = a_ref[...]
    for b in range(blocks):
        low, high = b * LANES, (b + 1) * LANES
        tiles = [work[low + t * GROUP:low + (t + 1) * GROUP, low:high] for t in range(LANES // GROUP)]
        inverse = jnp.concatenate(invert_diagonal(tiles), axis=0)
        parts = []
        if b > 0:
            parts.append(jnp.dot(inverse, work[low:high, :low], precision=exact, preferred_element_type=jnp.float32))
        parts.append(inverse)
        left = jnp.concatenate(parts, axis=1)
        w_ref[low:high, :high] = left
        if high < size:
            w_ref[low:high, high:] = jnp.zeros((LANES, size - high), jnp.float32)
            right = jnp.dot(inverse, work[low:high, high:], precision=exact, preferred_element_type=jnp.float32)
            work[high:, low:high] = jnp.zeros((size - high, LANES), jnp.float32)
            work[high:, :] -= lax.dot_general(
                right,
                jnp.concatenate([left, right], axis=1),
                (((0,), (0,)), ((), ())),
                precision=exact,
                preferred_element_type=jnp.float32,
            )


def inverse_factor(kernel_block):
    size = kernel_block.shape[0]
    return pl.pallas_call(
        inverse_kernel,
        out_shape=jax.ShapeDtypeStruct((size, size), jnp.float32),
        in_specs=[pl.BlockSpec(memory_space=pltpu.VMEM)],
        out_specs=pl.BlockSpec(memory_space=pltpu.VMEM),
        scratch_shapes=[pltpu.VMEM((size, size), jnp.float32)],
        compiler_params=pltpu.CompilerParams(vmem_limit_bytes=24 * MIB),
    )(kernel_block)


def per_device(points, prior, first_pivots, second_pivots):
    row_count, width = points.shape
    ranks = lax.axis_size("rank")
    block = first_pivots.shape[0]
    pivots = jnp.concatenate([first_pivots, second_pivots])
    first_id = lax.axis_index("pts") * row_count
    global_ids = first_id + lax.iota(jnp.int32, row_count)
    feature_count = width * ranks
    mine = jnp.concatenate(
        [owned_rows(prior, pivots, first_id), owned_rows(points, pivots, first_id)], axis=1
    )
    gathered = sum_over_points(mine)
    piv_factor, piv_wide = gathered[:, :-width], gathered[:, -width:]
    piv_x = piv_wide.astype(jnp.bfloat16)
    piv_norms = square_norms(piv_wide)
    row_norms = square_norms(points)

    def combine(rows, norms, factor, matches):
        distance = norms[:, None] + piv_norms[None, :] - 2.0 * contract(rows, piv_x)
        product = contract(factor, piv_factor, lax.Precision.HIGH)
        if ranks > 1:
            distance, product = lax.psum((distance, product), "rank")
        return jnp.exp(-distance / feature_count) + NUGGET * matches.astype(jnp.float32) - product

    kernel_block = combine(piv_x, piv_norms, piv_factor, jnp.eye(2 * block, dtype=jnp.float32))
    inverse = inverse_factor(kernel_block)
    panel = combine(points, row_norms, prior, global_ids[:, None] == pivots[None, :])
    own = block // ranks
    start = lax.axis_index("rank") * own
    first_inverse = lax.dynamic_slice_in_dim(inverse[:block, :block], start, own, 0)
    second_inverse = lax.dynamic_slice_in_dim(inverse[block:], start, own, 0)
    first_columns = contract(panel[:, :block], first_inverse, lax.Precision.HIGH)
    second_columns = contract(panel, second_inverse, lax.Precision.HIGH)
    return (first_columns, second_columns)


def solution(mesh):
    return jax.shard_map(
        per_device,
        mesh=mesh,
        in_specs=(P("pts", "rank"), P("pts", "rank"), P(), P()),
        out_specs=(P("pts", "rank"), P("pts", "rank")),
        check_vma=False,
    )
```

```python
import functools

import jax
import jax.numpy as jnp
from jax import lax
from jax.experimental import pallas as pl
from jax.experimental.pallas import tpu as pltpu
from jax.sharding import PartitionSpec as P

NUGGET = 2.0
LANES = 128
GROUP = 8
MIB = 1 << 20


def contract(left_rows, right_rows, precision=None):
    return lax.dot_general(
        left_rows,
        right_rows,
        (((1,), (1,)), ((), ())),
        precision=precision,
        preferred_element_type=jnp.float32,
    )


ROW_TILE = 16


def owned_kernel(pivots_ref, points_ref, prior_ref, mine_ref):
    row_count, width = points_ref.shape
    first_id = lax.axis_index("pts") * row_count
    mine_ref[...] = jnp.zeros_like(mine_ref)

    def group(g, carry):
        local = [pivots_ref[g * GROUP + k] - first_id for k in range(GROUP)]
        inside = [(index >= 0) & (index < row_count) for index in local]
        some = functools.reduce(jnp.logical_or, inside)

        @pl.when(some)
        def _():
            for k in range(GROUP):

                @pl.when(inside[k])
                def _():
                    target = pl.ds(g * GROUP + k, 1)
                    factor = prior_ref[pl.ds(local[k], 1), :]
                    start = pl.multiple_of((local[k] // ROW_TILE) * ROW_TILE, ROW_TILE)
                    near = points_ref[pl.ds(start, ROW_TILE), :].astype(jnp.float32)
                    place = lax.broadcasted_iota(jnp.int32, near.shape, 0)
                    picked = jnp.where(place == local[k] - start, near, 0.0)
                    features = jnp.sum(picked, axis=0, keepdims=True)
                    mine_ref[target, :] = jnp.concatenate([factor, features], axis=1)

        return carry

    lax.fori_loop(0, mine_ref.shape[0] // GROUP, group, 0)


def owned_rows(points, prior, pivots):
    columns = prior.shape[1] + points.shape[1]
    return pl.pallas_call(
        owned_kernel,
        out_shape=jax.ShapeDtypeStruct((pivots.shape[0], columns), jnp.float32),
        in_specs=[
            pl.BlockSpec(memory_space=pltpu.SMEM),
            pl.BlockSpec(memory_space=pltpu.VMEM),
            pl.BlockSpec(memory_space=pltpu.VMEM),
        ],
        out_specs=pl.BlockSpec(memory_space=pltpu.VMEM),
        compiler_params=pltpu.CompilerParams(vmem_limit_bytes=24 * MIB),
    )(pivots, points, prior)


def square_norms(values):
    wide = values.astype(jnp.float32)
    return jnp.sum(wide * wide, axis=1)


def chain_plan(bits, columns):
    tiles = columns // LANES
    middle = list(range(1, bits - 1))
    ways = max(1, min(len(middle), 3, tiles))
    edges = [LANES * (tiles * way // ways) for way in range(ways + 1)]
    plan = []
    for way in range(ways):
        order = [0] + middle[way:] + middle[:way] + [bits - 1]
        plan.append((order, edges[way], edges[way + 1]))
    return plan


def exchange_kernel(bits, plan, mine_ref, sum_ref, work, landed, send_sem, recv_sem):
    me, rank = lax.axis_index("pts"), lax.axis_index("rank")
    rows = sum_ref.shape[0]
    half_of = [(me // (1 << b)) % 2 for b in range(bits)]
    partner_of = [me + (1 - 2 * half_of[b]) * (1 << b) for b in range(bits)]

    barrier = pltpu.get_barrier_semaphore()
    for b in range(bits):
        pl.semaphore_signal(
            barrier, inc=1, device_id=(partner_of[b], rank), device_id_type=pl.DeviceIdType.MESH
        )
    pl.semaphore_wait(barrier, bits)

    def copy(source, target, b, step, way):
        return pltpu.make_async_remote_copy(
            src_ref=source,
            dst_ref=target,
            send_sem=send_sem.at[step, way],
            recv_sem=recv_sem.at[step, way],
            device_id=(partner_of[b], rank),
            device_id_type=pl.DeviceIdType.MESH,
        )

    starts = [0 for _ in plan]
    running = [None for _ in plan]
    unit = rows >> bits

    def begin_halving(way, step):
        order, left, right = plan[way]
        b, size = order[step], rows >> (step + 1)
        offset = rows - (rows >> step)
        away = pl.multiple_of(starts[way] + (1 - half_of[b]) * size, unit)
        source = work if step else mine_ref
        running[way] = copy(
            source.at[pl.ds(away, size), pl.ds(left, right - left)],
            landed.at[pl.ds(offset, size), pl.ds(left, right - left)],
            b, step, way,
        )
        running[way].start()

    def end_halving(way, step):
        order, left, right = plan[way]
        b, size = order[step], rows >> (step + 1)
        offset = rows - (rows >> step)
        running[way].wait()
        starts[way] = starts[way] + half_of[b] * size
        keep = pl.ds(pl.multiple_of(starts[way], unit), size)
        source = work if step else mine_ref
        target = work if step < bits - 1 else sum_ref
        target[keep, left:right] = source[keep, left:right] + landed[offset:offset + size, left:right]

    def begin_doubling(way, step):
        order, left, right = plan[way]
        b, size = order[step], rows >> (step + 1)
        block = sum_ref.at[pl.ds(pl.multiple_of(starts[way], unit), size), pl.ds(left, right - left)]
        running[way] = copy(block, block, b, 2 * bits - 1 - step, way)
        running[way].start()

    def end_doubling(way, step):
        order, left, right = plan[way]
        b, size = order[step], rows >> (step + 1)
        running[way].wait()
        starts[way] = starts[way] - half_of[b] * size

    ways = range(len(plan))
    for way in ways:
        begin_halving(way, 0)
    for step in range(bits):
        for way in ways:
            end_halving(way, step)
            if step < bits - 1:
                begin_halving(way, step + 1)
            else:
                begin_doubling(way, step)
    for step in reversed(range(bits)):
        for way in ways:
            end_doubling(way, step)
            if step > 0:
                begin_doubling(way, step - 1)


def sum_over_points(mine):
    count = lax.axis_size("pts")
    rows, columns = mine.shape
    bits = count.bit_length() - 1
    if count != 1 << bits or bits < 3 or rows % (8 * count) or columns % LANES:
        return lax.psum(mine, "pts")
    plan = chain_plan(bits, columns)
    return pl.pallas_call(
        functools.partial(exchange_kernel, bits, plan),
        out_shape=jax.ShapeDtypeStruct(mine.shape, jnp.float32),
        in_specs=[pl.BlockSpec(memory_space=pltpu.VMEM)],
        out_specs=pl.BlockSpec(memory_space=pltpu.VMEM),
        scratch_shapes=[
            pltpu.VMEM((rows, columns), jnp.float32),
            pltpu.VMEM((rows, columns), jnp.float32),
            pltpu.SemaphoreType.DMA((2 * bits, len(plan))),
            pltpu.SemaphoreType.DMA((2 * bits, len(plan))),
        ],
        compiler_params=pltpu.CompilerParams(
            collective_id=0, has_side_effects=True, vmem_limit_bytes=24 * MIB
        ),
    )(mine)


def invert_diagonal(tiles):
    count = len(tiles)
    tiles = list(tiles)
    sub = lax.broadcasted_iota(jnp.int32, (GROUP, LANES), 0)
    lane = lax.broadcasted_iota(jnp.int32, (GROUP, LANES), 1)
    result = []
    for g in range(count):
        base = g * GROUP
        rows = tiles[g]
        cols = [jnp.broadcast_to(rows[:, base + k:base + k + 1], (GROUP, LANES)) for k in range(GROUP)]
        in_group = (lane >= base) & (lane < base + GROUP)
        rows = jnp.where(in_group, jnp.where(lane == sub + base, 1.0, 0.0), rows)
        scale = jnp.zeros((GROUP, LANES), jnp.float32)
        ahead = g < count - 1
        if ahead:
            nearby = tiles[g + 1]
            below = [
                jnp.broadcast_to(nearby[:, base + k:base + k + 1], (GROUP, LANES)) for k in range(GROUP)
            ]
            nearby = jnp.where(in_group, 0.0, nearby)
        for k in range(GROUP):
            inv = 1.0 / jnp.broadcast_to(cols[k][k:k + 1, :], (GROUP, LANES))
            scale = jnp.where(sub == k, inv, scale)
            pivot_row = jnp.broadcast_to(rows[k:k + 1, :], (GROUP, LANES))
            heads = [jnp.broadcast_to(cols[j][k:k + 1, :], (GROUP, LANES)) for j in range(k + 1, GROUP)]
            if k < GROUP - 1:
                mult = jnp.where(sub > k, cols[k] * inv, 0.0)
                for j in range(k + 1, GROUP):
                    cols[j] = cols[j] - mult * heads[j - k - 1]
                rows = rows - mult * pivot_row
            if ahead:
                mult = below[k] * inv
                for j in range(k + 1, GROUP):
                    below[j] = below[j] - mult * heads[j - k - 1]
                nearby = nearby - mult * pivot_row
        result.append(jnp.where(lane <= sub + base, rows * jnp.sqrt(scale), 0.0))
        if ahead:
            tiles[g + 1] = nearby
        if g < count - 2:
            across = jnp.transpose(rows * scale)
            spread = [jnp.broadcast_to(rows[k:k + 1, :], (GROUP, LANES)) for k in range(GROUP)]
            for i in range(g + 2, count):
                part = across[i * GROUP:(i + 1) * GROUP, :]
                tile = jnp.where(in_group, 0.0, tiles[i])
                for k in range(GROUP):
                    tile = tile - jnp.broadcast_to(part[:, k:k + 1], (GROUP, LANES)) * spread[k]
                tiles[i] = tile
    return result


def inverse_kernel(a_ref, w_ref, work):
    size = a_ref.shape[0]
    blocks = size // LANES
    exact = lax.Precision.HIGHEST
    work[...] = a_ref[...]
    for b in range(blocks):
        low, high = b * LANES, (b + 1) * LANES
        tiles = [work[low + t * GROUP:low + (t + 1) * GROUP, low:high] for t in range(LANES // GROUP)]
        inverse = jnp.concatenate(invert_diagonal(tiles), axis=0)
        parts = []
        if b > 0:
            parts.append(jnp.dot(inverse, work[low:high, :low], precision=exact, preferred_element_type=jnp.float32))
        parts.append(inverse)
        left = jnp.concatenate(parts, axis=1)
        w_ref[low:high, :high] = left
        if high < size:
            w_ref[low:high, high:] = jnp.zeros((LANES, size - high), jnp.float32)
            right = jnp.dot(inverse, work[low:high, high:], precision=exact, preferred_element_type=jnp.float32)
            work[high:, low:high] = jnp.zeros((size - high, LANES), jnp.float32)
            work[high:, :] -= lax.dot_general(
                right,
                jnp.concatenate([left, right], axis=1),
                (((0,), (0,)), ((), ())),
                precision=exact,
                preferred_element_type=jnp.float32,
            )


def inverse_factor(kernel_block):
    size = kernel_block.shape[0]
    return pl.pallas_call(
        inverse_kernel,
        out_shape=jax.ShapeDtypeStruct((size, size), jnp.float32),
        in_specs=[pl.BlockSpec(memory_space=pltpu.VMEM)],
        out_specs=pl.BlockSpec(memory_space=pltpu.VMEM),
        scratch_shapes=[pltpu.VMEM((size, size), jnp.float32)],
        compiler_params=pltpu.CompilerParams(vmem_limit_bytes=24 * MIB),
    )(kernel_block)


def per_device(points, prior, first_pivots, second_pivots):
    row_count, width = points.shape
    ranks = lax.axis_size("rank")
    block = first_pivots.shape[0]
    pivots = jnp.concatenate([first_pivots, second_pivots])
    first_id = lax.axis_index("pts") * row_count
    global_ids = first_id + lax.iota(jnp.int32, row_count)
    feature_count = width * ranks
    mine = owned_rows(points, prior, pivots)
    gathered = sum_over_points(mine)
    piv_factor, piv_wide = gathered[:, :-width], gathered[:, -width:]
    piv_x = piv_wide.astype(jnp.bfloat16)
    piv_norms = square_norms(piv_wide)
    row_norms = square_norms(points)

    def combine(rows, norms, factor, matches):
        distance = norms[:, None] + piv_norms[None, :] - 2.0 * contract(rows, piv_x)
        product = contract(factor, piv_factor, lax.Precision.HIGH)
        if ranks > 1:
            distance, product = lax.psum((distance, product), "rank")
        return jnp.exp(-distance / feature_count) + NUGGET * matches.astype(jnp.float32) - product

    kernel_block = combine(piv_x, piv_norms, piv_factor, jnp.eye(2 * block, dtype=jnp.float32))
    inverse = inverse_factor(kernel_block)
    panel = combine(points, row_norms, prior, global_ids[:, None] == pivots[None, :])
    own = block // ranks
    start = lax.axis_index("rank") * own
    first_inverse = lax.dynamic_slice_in_dim(inverse[:block, :block], start, own, 0)
    second_inverse = lax.dynamic_slice_in_dim(inverse[block:], start, own, 0)
    first_columns = contract(panel[:, :block], first_inverse, lax.Precision.HIGH)
    second_columns = contract(panel, second_inverse, lax.Precision.HIGH)
    return (first_columns, second_columns)


def solution(mesh):
    return jax.shard_map(
        per_device,
        mesh=mesh,
        in_specs=(P("pts", "rank"), P("pts", "rank"), P(), P()),
        out_specs=(P("pts", "rank"), P("pts", "rank")),
        check_vma=False,
    )
```
